512 devices in a mesh: seq: 32 (over y, x, core), head: 16 (over z).
Axes of the slice: x: 4, y: 4, z: 16, core: 2. Of those that a mesh axis runs over, the one named last changes fastest.
Arguments:
- queries: bfloat16 [65536, 2048], P('seq', 'head'), may hold values from -6 to 6
- keys: bfloat16 [65536, 2048], P('seq', 'head'), may hold values from -6 to 6
- values: bfloat16 [65536, 2048], P('seq', 'head'), may hold values from -6 to 6
- level_ids: int32 [65536], P('seq'), may hold values from 0 to 63
- level_table: float32 [64, 17], replicated, may hold values from 0 to 4, as said below
- out_cotangent: bfloat16 [65536, 2048], P('seq', 'head'), may hold values from -6 to 6
Outputs:
- attn_out: bfloat16 [65536, 2048], P('seq', 'head')
- weight_grad: float32 [2048, 2048], P('seq', 'head')
The draws below stay inside these ranges and needn't reach their ends.
Inputs may be any that keep to these rules, and one draw needn't show every extreme that they name: `level_table`: positive coefficients.
All inputs are finite; a program needn't handle non-finite values.
Results may differ from the reference program's by a relative error of at most 0.0043.
Values may be sent and summed in bfloat16 or wider, within the bound.
No kernel may reach another device: no remote copies, remote signals or barrier semaphores. Data moves between devices by JAX's collectives and lax.ppermute only.
A program may use at most 64 MiB of HBM per device.

```python
import jax
import jax.numpy as jnp
from jax import lax

D = 2048
HD = 128
NID = 64
TOK_DEV = 2048
HEADS = 16
TOKENS = 65536
LOCAL_BITS = 11
SEQ_BITS = 5
LEVELS = 17
N_SEQ = 32


def draw_level_table(key, part):
    spread = jax.random.uniform(key, (NID, LEVELS), jnp.float32, -0.7, 0.7)
    level_depth = jnp.maximum(jnp.arange(LEVELS) - 1, 0).astype(jnp.float32)
    return jnp.exp(spread) * jnp.exp2(-0.5 * level_depth)[None, :]


def plant(entries, stream_key, low, largest):
    place = [jax.random.randint(jax.random.fold_in(stream_key, axis), (), 0, length) for axis, length in enumerate(entries.shape)]
    longest = entries.shape.index(max(entries.shape))
    next_to = place[:longest] + [(place[longest] + 1) % entries.shape[longest]] + place[longest + 1:]
    return entries.at[tuple(place)].set(low).at[tuple(next_to)].set(largest)


def with_spikes(values, key, source, target, blocks, factor):
    def block_of(dim):
        return (jnp.arange(values.shape[dim]) // (values.shape[dim] // blocks)).reshape((-1,) + (1,) * (values.ndim - 1 - dim))

    near = jax.random.permutation(key, blocks)[block_of(target)]
    second = (block_of(target) + blocks // 2) % blocks
    return jnp.where((block_of(source) == near) | (block_of(source) == second), factor * values, values)


def level_of(stream_key, dims, pieces, low, high):
    def one(dim, blocks):
        draws = jax.random.uniform(jax.random.fold_in(jax.random.fold_in(stream_key, 6), dim), (blocks,), jnp.float32, low / len(pieces), high / len(pieces))
        return jnp.repeat(jnp.exp(draws), dims[dim] // blocks).reshape((-1,) + (1,) * (len(dims) - dim - 1))

    factor_of = one(*pieces[0])
    for cut in pieces[1:]:
        factor_of = factor_of * one(*cut)
    return factor_of


def scatter_about(stream_key, dims, deviation, bound, cuts=(), kind=jnp.bfloat16):
    values = deviation * jax.random.normal(stream_key, dims, jnp.float32)
    if cuts:
        values = values * level_of(stream_key, dims, cuts, -0.22, 0.18)
    return jnp.clip(values, -bound, bound).astype(kind)


def bell_draw_with(rng, shape, width, most, split, heavy, held_as=jnp.bfloat16):
    result = width * jax.random.normal(rng, shape, jnp.float32)
    if split:
        result = result * level_of(rng, shape, split, -0.22, 0.18)
    return jnp.clip(with_spikes(result, jax.random.fold_in(rng, 3), *heavy), -most, most).astype(held_as)


def setup_inputs(seed: int = 0) -> dict:
    arg_keys = jax.random.split(jax.random.key(seed), 7)
    queries = scatter_about(arg_keys[0], (TOKENS, HEADS * HD), 1.0, 6.0, ((0, 32), (1, 16)))
    keys = scatter_about(arg_keys[1], (TOKENS, HEADS * HD), 1.0, 6.0, ((0, 32), (1, 16)))
    values = scatter_about(arg_keys[2], (TOKENS, HEADS * HD), 1.0, 6.0, ((0, 32), (1, 16)))
    level_ids = plant(jax.random.randint(arg_keys[3], (TOKENS,), 0, NID), jax.random.fold_in(arg_keys[3], 1), 0, NID - 1).astype(jnp.int32)
    level_table = draw_level_table(jax.random.fold_in(arg_keys[6], 71), 0)
    out_cotangent = bell_draw_with(arg_keys[5], (TOKENS, D), 1.0, 6.0, ((0, 32), (1, 16)), (0, 1, 32, 2.75))
    return dict(queries=queries, keys=keys, values=values, level_ids=level_ids, level_table=level_table, out_cotangent=out_cotangent)


EPSILON = 1e-06
HIGHEST = lax.Precision.HIGHEST

def level_index(row_pos, col_pos, bit_count):
    xor_value = jnp.bitwise_xor(row_pos, col_pos)
    levels = jnp.zeros(xor_value.shape, jnp.int32)
    for shift_by in range(bit_count):
        levels = levels + (jnp.right_shift(xor_value, shift_by) > 0).astype(jnp.int32)
    return levels

def split_heads(array):
    return array.reshape(N_SEQ, TOK_DEV, HEADS, HD).transpose(2, 0, 1, 3)

def reference(queries, keys, values, level_ids, level_table, out_cotangent):
    coeff = level_table[level_ids].reshape(N_SEQ, TOK_DEV, LEVELS)
    position = jnp.arange(TOK_DEV, dtype=jnp.int32)
    levels = level_index(position[:, None], position[None, :], LOCAL_BITS)
    causal = position[None, :] <= position[:, None]

    def block_weights(block_coeff):
        weights = jnp.zeros((TOK_DEV, TOK_DEV), jnp.float32)
        for level in range(LOCAL_BITS + 1):
            weights = weights + jnp.where(levels == level, block_coeff[:, level:level + 1], 0.0)
        return jnp.where(causal, weights, 0.0)
    all_weights = lax.map(block_weights, coeff)
    owner = jnp.arange(N_SEQ, dtype=jnp.int32)
    apart = jnp.bitwise_xor(owner[:, None], owner[None, :])
    earlier = owner[None, :] < owner[:, None]
    sibling = jnp.stack([((jnp.right_shift(apart, level) == 1) & earlier).astype(jnp.float32) for level in range(SEQ_BITS)])
    cross_coeff = coeff[:, :, LOCAL_BITS + 1:]

    def one_head(parts):
        query_blocks, key_blocks, value_blocks = parts

        def one_block(items):
            query, key_block, value, weights = items
            scores = jnp.dot(query, key_block.T, preferred_element_type=jnp.float32)
            mixed = (weights * scores).astype(jnp.bfloat16)
            local = jnp.dot(mixed, value, preferred_element_type=jnp.float32)
            state = jnp.dot(key_block.T, value, preferred_element_type=jnp.float32)
            return (local, state)
        local, states = lax.map(one_block, (query_blocks, key_blocks, value_blocks, all_weights))
        level_states = jnp.einsum('jcb,bde->jcde', sibling, states, precision=HIGHEST)
        readout = jnp.einsum('cti,jcie->ctje', query_blocks.astype(jnp.float32), level_states, precision=HIGHEST)
        cross = lax.optimization_barrier(jnp.sum(readout * cross_coeff[:, :, :, None], axis=2))
        total = local + cross
        normed = total * lax.rsqrt(lax.optimization_barrier(jnp.mean(total * total, axis=-1, keepdims=True)) + EPSILON)
        return normed.astype(jnp.bfloat16)
    heads_out = lax.map(one_head, (split_heads(queries), split_heads(keys), split_heads(values)))
    attn_out = heads_out.transpose(1, 2, 0, 3).reshape(TOKENS, HEADS * HD)
    weight_grad = jnp.dot(out_cotangent.T, attn_out, preferred_element_type=jnp.float32) * TOKENS ** (-0.5)
    return (attn_out, weight_grad)
```

```python
import functools

import jax
import jax.numpy as jnp
from jax import lax
from jax.experimental import pallas as pl
from jax.experimental.pallas import tpu as pltpu
from jax.sharding import PartitionSpec as P

EPSILON = 1e-06
HIGHEST = lax.Precision.HIGHEST
PIECE = 512
TILE = 128
RING_ROWS = 40
STREAMS = 1


def dot_t(a, b):
    return lax.dot_general(a, b, (((1,), (1,)), ((), ())), preferred_element_type=jnp.float32)


def dot(a, b):
    return jnp.dot(a, b, preferred_element_type=jnp.float32)


def local_kernel(piece, q_ref, k_ref, v_ref, c_ref, out_ref):
    base = piece * PIECE
    piece_bits = PIECE.bit_length() - 1
    tile_bits = TILE.bit_length() - 1
    q = q_ref[...]
    total = jnp.zeros((PIECE, q.shape[1]), jnp.float32)
    first = 0
    for bit in reversed(range(max(piece.bit_length(), 1))):
        if not (piece >> bit) & 1:
            continue
        last = first + (PIECE << bit)
        level = piece_bits + bit + 1
        scores = dot_t(q, k_ref[first:last, :])
        mixed = (scores * c_ref[:, level : level + 1]).astype(jnp.bfloat16)
        total = total + dot(mixed, v_ref[first:last, :])
        first = last
    out_ref[...] = total
    for bit in reversed(range(piece_bits - tile_bits)):
        half = TILE << bit
        level = tile_bits + bit + 1
        for start in range(0, PIECE, 2 * half):
            rows = slice(start + half, start + 2 * half)
            cols = slice(base + start, base + start + half)
            scores = dot_t(q_ref[rows, :], k_ref[cols, :])
            mixed = (scores * c_ref[rows, level : level + 1]).astype(jnp.bfloat16)
            out_ref[rows, :] += dot(mixed, v_ref[cols, :])
    row = lax.broadcasted_iota(jnp.int32, (TILE, TILE), 0)
    col = lax.broadcasted_iota(jnp.int32, (TILE, TILE), 1)
    apart = jnp.bitwise_xor(row, col)
    causal = col <= row
    for start in range(0, PIECE, TILE):
        rows = slice(start, start + TILE)
        cols = slice(base + start, base + start + TILE)
        weights = jnp.broadcast_to(c_ref[rows, 0:1], (TILE, TILE))
        for level in range(1, tile_bits + 1):
            weights = jnp.where(apart >= 1 << (level - 1), c_ref[rows, level : level + 1], weights)
        weights = jnp.where(causal, weights, 0.0)
        mixed = (dot_t(q_ref[rows, :], k_ref[cols, :]) * weights).astype(jnp.bfloat16)
        out_ref[rows, :] += dot(mixed, v_ref[cols, :])


def local_piece(piece, queries, keys, values, coeff):
    head_dim = queries.shape[1]
    upto = (piece + 1) * PIECE
    levels = coeff.shape[1]
    return pl.pallas_call(
        functools.partial(local_kernel, piece),
        out_shape=jax.ShapeDtypeStruct((PIECE, head_dim), jnp.float32),
        grid=(1,),
        in_specs=[
            pl.BlockSpec((PIECE, head_dim), lambda i: (piece, 0)),
            pl.BlockSpec((upto, head_dim), lambda i: (0, 0)),
            pl.BlockSpec((upto, head_dim), lambda i: (0, 0)),
            pl.BlockSpec((PIECE, levels), lambda i: (piece, 0)),
        ],
        out_specs=pl.BlockSpec((PIECE, head_dim), lambda i: (0, 0)),
        compiler_params=pltpu.CompilerParams(vmem_limit_bytes=32 * 1024 * 1024),
        cost_estimate=pl.CostEstimate(
            flops=4 * PIECE * upto * head_dim, bytes_accessed=4 * upto * head_dim, transcendentals=0
        ),
    )(queries, keys, values, coeff)


def finish_kernel(first_level, seq_bits, l0, l1, l2, l3, q_ref, c_ref, hi_ref, lo_ref, out_ref):
    locals_ = (l0, l1, l2, l3)
    for piece in range(4):
        rows = slice(piece * PIECE, (piece + 1) * PIECE)
        q = q_ref[rows, :]
        total = locals_[piece][...]
        cross = jnp.zeros_like(total)
        for j in range(seq_bits):
            readout = dot(q, hi_ref[j]) + dot(q, lo_ref[j])
            level = first_level + j
            cross = cross + readout * c_ref[rows, level : level + 1]
        total = total + cross
        mean = jnp.mean(total * total, axis=1, keepdims=True)
        out_ref[rows, :] = (total * lax.rsqrt(mean + EPSILON)).astype(jnp.bfloat16)


def finish(pieces, queries, coeff, states, first_level):
    hi = states.astype(jnp.bfloat16)
    lo = (states - hi.astype(jnp.float32)).astype(jnp.bfloat16)
    return pl.pallas_call(
        functools.partial(finish_kernel, first_level, states.shape[0]),
        out_shape=jax.ShapeDtypeStruct(queries.shape, jnp.bfloat16),
        compiler_params=pltpu.CompilerParams(vmem_limit_bytes=32 * 1024 * 1024),
        cost_estimate=pl.CostEstimate(
            flops=20 * queries.shape[0] * 128 * 128, bytes_accessed=4 << 20, transcendentals=0
        ),
    )(*pieces, queries, coeff, hi, lo)


def ring_gather(shard, axis, streams):
    size = lax.axis_size(axis)
    right = [(i, (i + 1) % size) for i in range(size)]
    left = [(i, (i - 1) % size) for i in range(size)]
    rows = shard.shape[0] // streams
    parts = []
    for stream in range(streams):
        own = shard[stream * rows : (stream + 1) * rows]
        arrived = {0: own}
        up, down = own, own
        for step in range(1, size // 2):
            up = lax.ppermute(up, axis, right)
            down = lax.ppermute(down, axis, left)
            arrived[size - step] = up
            arrived[step] = down
        if stream % 2 == 0:
            arrived[size // 2] = lax.ppermute(up, axis, right)
        else:
            arrived[size // 2] = lax.ppermute(down, axis, left)
        parts.append([arrived[k] for k in range(size)])
    return parts


def body(queries, keys, values, level_ids, level_table, out_cotangent):
    block_len, head_dim = queries.shape
    n_seq = lax.axis_size("seq")
    n_head = lax.axis_size("head")
    local_bits = block_len.bit_length() - 1
    seq_bits = n_seq.bit_length() - 1
    table_rows = level_table.shape[0]
    own_index = lax.axis_index("seq")
    own_head = lax.axis_index("head")

    cot = out_cotangent.T.reshape(2, head_dim // 2, block_len)
    ring_part = cot[:, :RING_ROWS].reshape(2 * RING_ROWS, block_len)
    gather_part = cot[:, RING_ROWS:].reshape(head_dim - 2 * RING_ROWS, block_len)
    gathered = lax.all_gather(gather_part, "head", axis=0)
    ring = ring_gather(ring_part, "head", STREAMS)

    state = lax.dot_general(
        keys, values, (((0,), (0,)), ((), ())), preferred_element_type=jnp.float32
    )
    states = lax.all_to_all(
        jnp.broadcast_to(state, (n_seq, head_dim, head_dim)), "seq", 0, 0, tiled=True
    )
    source = jnp.arange(n_seq, dtype=jnp.int32)
    apart = jnp.bitwise_xor(own_index, source)
    select = jnp.stack(
        [
            ((jnp.right_shift(apart, level) == 1) & (source < own_index)).astype(jnp.float32)
            for level in range(seq_bits)
        ]
    )
    level_states = jnp.einsum("ji,ide->jde", select, states, precision=HIGHEST)

    onehot = (level_ids[:, None] == jnp.arange(table_rows, dtype=jnp.int32)[None, :]).astype(
        jnp.float32
    )
    coeff = jnp.dot(onehot, level_table, precision=HIGHEST, preferred_element_type=jnp.float32)
    pieces = [
        local_piece(piece, queries, keys, values, coeff) for piece in range(block_len // PIECE)
    ]
    attn_out = finish(pieces, queries, coeff, level_states, local_bits + 1)

    scale = (block_len * n_seq) ** (-0.5)

    def own_share(products):
        rows = products.shape[2]
        sent = products.reshape(n_seq, rows, head_dim).astype(jnp.bfloat16)
        arrived = lax.all_to_all(sent, "seq", 0, 0, tiled=True)
        return arrived.astype(jnp.float32).sum(axis=0) * scale

    streams = []
    for parts in ring:
        products = jnp.stack([dot(part, attn_out) for part in parts])
        doubled = jnp.concatenate([products, products], axis=0).astype(jnp.bfloat16)
        streams.append(lax.dynamic_slice_in_dim(doubled, n_head - own_head, n_head, 0))
    products = jnp.concatenate(streams, axis=1).reshape(n_head, 2, RING_ROWS, head_dim)
    upper = own_share(products)
    rest = dot(gathered.reshape(-1, block_len), attn_out)
    lower = own_share(rest.reshape(n_head, 2, head_dim // 2 - RING_ROWS, head_dim))
    return attn_out, jnp.concatenate([upper, lower], axis=0)


def solution(mesh):
    in_specs = (
        P("seq", "head"),
        P("seq", "head"),
        P("seq", "head"),
        P("seq"),
        P(),
        P("seq", "head"),
    )
    out_specs = (P("seq", "head"), P("seq", "head"))
    return jax.shard_map(body, mesh=mesh, in_specs=in_specs, out_specs=out_specs, check_vma=False)
```

```python
import functools

import jax
import jax.numpy as jnp
from jax import lax
from jax.experimental import pallas as pl
from jax.experimental.pallas import tpu as pltpu
from jax.sharding import PartitionSpec as P

EPSILON = 1e-06
HIGHEST = lax.Precision.HIGHEST
PIECE = 512
TILE = 128
GROUP = 2


def dot_t(a, b):
    return lax.dot_general(a, b, (((1,), (1,)), ((), ())), preferred_element_type=jnp.float32)


def dot(a, b):
    return jnp.dot(a, b, preferred_element_type=jnp.float32)


def local_kernel(piece, q_ref, k_ref, v_ref, c_ref, out_ref):
    base = piece * PIECE
    piece_bits = PIECE.bit_length() - 1
    tile_bits = TILE.bit_length() - 1
    q = q_ref[...]
    total = jnp.zeros((PIECE, q.shape[1]), jnp.float32)
    first = 0
    for bit in reversed(range(max(piece.bit_length(), 1))):
        if not (piece >> bit) & 1:
            continue
        last = first + (PIECE << bit)
        level = piece_bits + bit + 1
        scores = dot_t(q, k_ref[first:last, :])
        mixed = (scores * c_ref[:, level : level + 1]).astype(jnp.bfloat16)
        total = total + dot(mixed, v_ref[first:last, :])
        first = last
    out_ref[...] = total
    for bit in reversed(range(piece_bits - tile_bits)):
        half = TILE << bit
        level = tile_bits + bit + 1
        for start in range(0, PIECE, 2 * half):
            rows = slice(start + half, start + 2 * half)
            cols = slice(base + start, base + start + half)
            scores = dot_t(q_ref[rows, :], k_ref[cols, :])
            mixed = (scores * c_ref[rows, level : level + 1]).astype(jnp.bfloat16)
            out_ref[rows, :] += dot(mixed, v_ref[cols, :])
    row = lax.broadcasted_iota(jnp.int32, (TILE, TILE), 0)
    col = lax.broadcasted_iota(jnp.int32, (TILE, TILE), 1)
    apart = jnp.bitwise_xor(row, col)
    causal = col <= row
    for start in range(0, PIECE, TILE):
        rows = slice(start, start + TILE)
        cols = slice(base + start, base + start + TILE)
        weights = jnp.broadcast_to(c_ref[rows, 0:1], (TILE, TILE))
        for level in range(1, tile_bits + 1):
            weights = jnp.where(apart >= 1 << (level - 1), c_ref[rows, level : level + 1], weights)
        weights = jnp.where(causal, weights, 0.0)
        mixed = (dot_t(q_ref[rows, :], k_ref[cols, :]) * weights).astype(jnp.bfloat16)
        out_ref[rows, :] += dot(mixed, v_ref[cols, :])


def local_piece(piece, queries, keys, values, coeff):
    head_dim = queries.shape[1]
    upto = (piece + 1) * PIECE
    levels = coeff.shape[1]
    return pl.pallas_call(
        functools.partial(local_kernel, piece),
        out_shape=jax.ShapeDtypeStruct((PIECE, head_dim), jnp.float32),
        grid=(1,),
        in_specs=[
            pl.BlockSpec((PIECE, head_dim), lambda i: (piece, 0)),
            pl.BlockSpec((upto, head_dim), lambda i: (0, 0)),
            pl.BlockSpec((upto, head_dim), lambda i: (0, 0)),
            pl.BlockSpec((PIECE, levels), lambda i: (piece, 0)),
        ],
        out_specs=pl.BlockSpec((PIECE, head_dim), lambda i: (0, 0)),
        compiler_params=pltpu.CompilerParams(vmem_limit_bytes=32 * 1024 * 1024),
        cost_estimate=pl.CostEstimate(
            flops=4 * PIECE * upto * head_dim, bytes_accessed=4 * upto * head_dim, transcendentals=0
        ),
    )(queries, keys, values, coeff)


def finish_kernel(first_level, seq_bits, l0, l1, l2, l3, q_ref, c_ref, hi_ref, lo_ref, out_ref):
    locals_ = (l0, l1, l2, l3)
    for piece in range(4):
        rows = slice(piece * PIECE, (piece + 1) * PIECE)
        q = q_ref[rows, :]
        total = locals_[piece][...]
        cross = jnp.zeros_like(total)
        for j in range(seq_bits):
            readout = dot(q, hi_ref[j]) + dot(q, lo_ref[j])
            level = first_level + j
            cross = cross + readout * c_ref[rows, level : level + 1]
        total = total + cross
        mean = jnp.mean(total * total, axis=1, keepdims=True)
        out_ref[rows, :] = (total * lax.rsqrt(mean + EPSILON)).astype(jnp.bfloat16)


def finish(pieces, queries, coeff, states, first_level):
    hi = states.astype(jnp.bfloat16)
    lo = (states - hi.astype(jnp.float32)).astype(jnp.bfloat16)
    return pl.pallas_call(
        functools.partial(finish_kernel, first_level, states.shape[0]),
        out_shape=jax.ShapeDtypeStruct(queries.shape, jnp.bfloat16),
        compiler_params=pltpu.CompilerParams(vmem_limit_bytes=32 * 1024 * 1024),
        cost_estimate=pl.CostEstimate(
            flops=20 * queries.shape[0] * 128 * 128, bytes_accessed=4 << 20, transcendentals=0
        ),
    )(*pieces, queries, coeff, hi, lo)


def exchange(value):
    size = lax.axis_size("zl")
    own = lax.axis_index("zl")
    rows = value.shape[0] // size
    slots = [lax.dynamic_slice_in_dim(value, own * rows, rows, 0)]
    for apart in range(1, size):
        to = lax.rem(own + apart, size)
        piece = lax.dynamic_slice_in_dim(value, to * rows, rows, 0)
        slots.append(lax.ppermute(piece, "zl", [(i, (i + apart) % size) for i in range(size)]))
    return slots


def ring_gather(own):
    size = lax.axis_size("zh")
    right = [(i, (i + 1) % size) for i in range(size)]
    left = [(i, (i - 1) % size) for i in range(size)]
    half = own.shape[0] // 2
    arrived = []
    up, down = own, own
    for step in range(1, size // 2):
        up = lax.ppermute(up, "zh", right)
        down = lax.ppermute(down, "zh", left)
        arrived += [(size - step, 0, up), (step, 0, down)]
    arrived.append((size // 2, 0, lax.ppermute(up[:half], "zh", right)))
    arrived.append((size // 2, half, lax.ppermute(down[half:], "zh", left)))
    return arrived


def product_store(place, count, blocks, zh, zl, a_refs, b_refs, store):
    b = jnp.concatenate([ref[...] for ref in b_refs], axis=1)
    for (away, first, slots), a_ref in zip(blocks, a_refs):
        group = lax.rem(zh + away, count)
        for slot in range(slots):
            a = a_ref[slot]
            product = lax.dot_general(
                a, b, (((0,), (0,)), ((), ())), preferred_element_type=jnp.float32
            ).astype(jnp.bfloat16)
            block = group * place + lax.rem(zl - (first + slot) + place, place)
            store(block, product)


def early_kernel(place, count, blocks, where_ref, *refs):
    b_refs, a_refs, out_ref = refs[:place], refs[place:-1], refs[-1]
    done = [0]

    def store(block, product):
        out_ref[done[0]] = product
        done[0] += 1

    product_store(place, count, blocks, where_ref[0], where_ref[1], a_refs, b_refs, store)


def late_kernel(place, count, early_blocks, blocks, where_ref, early_ref, *refs):
    b_refs, a_refs, out_ref = refs[:place], refs[place:-1], refs[-1]
    zh, zl = where_ref[0], where_ref[1]
    width = out_ref.shape[-1]
    rows = out_ref.shape[-2]

    def store(block, product):
        for half in range(2):
            for d in range(place):
                head = lax.rem(zl - d + place, place)
                out_ref[block, half, head] = product[
                    half * rows : (half + 1) * rows, d * width : (d + 1) * width
                ]

    done = 0
    for away, first, slots in early_blocks:
        group = lax.rem(zh + away, count)
        for slot in range(slots):
            block = group * place + lax.rem(zl - (first + slot) + place, place)
            store(block, early_ref[done])
            done += 1
    product_store(place, count, blocks, zh, zl, a_refs, b_refs, store)


def product_cost(blocks, shape, place):
    count = sum(slots for _, _, slots in blocks)
    rows, width = shape
    return pl.CostEstimate(
        flops=2 * count * rows * width * width * place,
        bytes_accessed=2 * rows * width * (count + place),
        transcendentals=0,
    )


def products(early, late, b_slots, zh_count):
    place = len(b_slots)
    rows, width = b_slots[0].shape
    where = jnp.stack([lax.axis_index("zh"), lax.axis_index("zl")]).astype(jnp.int32)
    early_blocks = [(away, first, a.shape[0]) for away, first, a in early]
    late_blocks = [(away, first, a.shape[0]) for away, first, a in late]
    count = sum(slots for _, _, slots in early_blocks)
    smem = pl.BlockSpec(memory_space=pltpu.SMEM)
    vmem = pl.BlockSpec(memory_space=pltpu.VMEM)
    params = pltpu.CompilerParams(vmem_limit_bytes=40 * 1024 * 1024)
    first = pl.pallas_call(
        functools.partial(early_kernel, place, zh_count, early_blocks),
        out_shape=jax.ShapeDtypeStruct((count, width, place * width), jnp.bfloat16),
        in_specs=[smem] + [vmem] * (place + len(early)),
        out_specs=vmem,
        compiler_params=params,
        cost_estimate=product_cost(early_blocks, (rows, width), place),
    )(where, *b_slots, *[a for _, _, a in early])
    return pl.pallas_call(
        functools.partial(late_kernel, place, zh_count, early_blocks, late_blocks),
        out_shape=jax.ShapeDtypeStruct(
            (zh_count * place, 2, place, width // 2, width), jnp.bfloat16
        ),
        in_specs=[smem] + [vmem] * (1 + place + len(late)),
        out_specs=vmem,
        compiler_params=params,
        cost_estimate=product_cost(late_blocks, (rows, width), place),
    )(where, first, *b_slots, *[a for _, _, a in late])


def body(queries, keys, values, level_ids, level_table, out_cotangent):
    block_len, head_dim = queries.shape
    n_seq = lax.axis_size("seq")
    local_bits = block_len.bit_length() - 1
    seq_bits = n_seq.bit_length() - 1
    table_rows = level_table.shape[0]
    own_index = lax.axis_index("seq")

    own = jnp.stack(exchange(out_cotangent))
    blocks = [(0, 0, own)] + ring_gather(own)

    state = lax.dot_general(
        keys, values, (((0,), (0,)), ((), ())), preferred_element_type=jnp.float32
    )
    states = lax.all_to_all(
        jnp.broadcast_to(state, (n_seq, head_dim, head_dim)), "seq", 0, 0, tiled=True
    )
    source = jnp.arange(n_seq, dtype=jnp.int32)
    apart = jnp.bitwise_xor(own_index, source)
    select = jnp.stack(
        [
            ((jnp.right_shift(apart, level) == 1) & (source < own_index)).astype(jnp.float32)
            for level in range(seq_bits)
        ]
    )
    level_states = jnp.einsum("ji,ide->jde", select, states, precision=HIGHEST)

    onehot = (level_ids[:, None] == jnp.arange(table_rows, dtype=jnp.int32)[None, :]).astype(
        jnp.float32
    )
    coeff = jnp.dot(onehot, level_table, precision=HIGHEST, preferred_element_type=jnp.float32)
    pieces = [
        local_piece(piece, queries, keys, values, coeff) for piece in range(block_len // PIECE)
    ]
    attn_out = finish(pieces, queries, coeff, level_states, local_bits + 1)

    scale = (block_len * n_seq) ** (-0.5)
    late = 4
    partial = products(blocks[:-late], blocks[-late:], exchange(attn_out), lax.axis_size("zh"))
    sent = partial.reshape(-1, head_dim // 2, head_dim)
    arrived = lax.all_to_all(sent, ("seq", "zl"), 0, 0, tiled=True)
    weight_grad = arrived.astype(jnp.float32).sum(axis=0) * scale
    return attn_out, weight_grad


def solution(mesh):
    n_seq, n_head = mesh.devices.shape
    mesh = jax.sharding.Mesh(
        mesh.devices.reshape(n_seq, n_head // GROUP, GROUP), ("seq", "zh", "zl")
    )
    split = P("seq", ("zh", "zl"))
    return jax.shard_map(
        body,
        mesh=mesh,
        in_specs=(split, split, split, P("seq"), P(), split),
        out_specs=(split, split),
        check_vma=False,
    )
```

```python
import functools

import jax
import jax.numpy as jnp
from jax import lax
from jax.experimental import pallas as pl
from jax.experimental.pallas import tpu as pltpu
from jax.sharding import PartitionSpec as P

EPSILON = 1e-06
HIGHEST = lax.Precision.HIGHEST
PIECE = 512
TILE = 128
GROUP = 4


def dot_t(a, b):
    return lax.dot_general(a, b, (((1,), (1,)), ((), ())), preferred_element_type=jnp.float32)


def dot(a, b):
    return jnp.dot(a, b, preferred_element_type=jnp.float32)


def local_kernel(piece, q_ref, k_ref, v_ref, c_ref, out_ref):
    base = piece * PIECE
    piece_bits = PIECE.bit_length() - 1
    tile_bits = TILE.bit_length() - 1
    q = q_ref[...]
    total = jnp.zeros((PIECE, q.shape[1]), jnp.float32)
    first = 0
    for bit in reversed(range(max(piece.bit_length(), 1))):
        if not (piece >> bit) & 1:
            continue
        last = first + (PIECE << bit)
        level = piece_bits + bit + 1
        scores = dot_t(q, k_ref[first:last, :])
        mixed = (scores * c_ref[:, level : level + 1]).astype(jnp.bfloat16)
        total = total + dot(mixed, v_ref[first:last, :])
        first = last
    out_ref[...] = total
    for bit in reversed(range(piece_bits - tile_bits)):
        half = TILE << bit
        level = tile_bits + bit + 1
        for start in range(0, PIECE, 2 * half):
            rows = slice(start + half, start + 2 * half)
            cols = slice(base + start, base + start + half)
            scores = dot_t(q_ref[rows, :], k_ref[cols, :])
            mixed = (scores * c_ref[rows, level : level + 1]).astype(jnp.bfloat16)
            out_ref[rows, :] += dot(mixed, v_ref[cols, :])
    row = lax.broadcasted_iota(jnp.int32, (TILE, TILE), 0)
    col = lax.broadcasted_iota(jnp.int32, (TILE, TILE), 1)
    apart = jnp.bitwise_xor(row, col)
    causal = col <= row
    for start in range(0, PIECE, TILE):
        rows = slice(start, start + TILE)
        cols = slice(base + start, base + start + TILE)
        weights = jnp.broadcast_to(c_ref[rows, 0:1], (TILE, TILE))
        for level in range(1, tile_bits + 1):
            weights = jnp.where(apart >= 1 << (level - 1), c_ref[rows, level : level + 1], weights)
        weights = jnp.where(causal, weights, 0.0)
        mixed = (dot_t(q_ref[rows, :], k_ref[cols, :]) * weights).astype(jnp.bfloat16)
        out_ref[rows, :] += dot(mixed, v_ref[cols, :])


def local_piece(piece, queries, keys, values, coeff):
    head_dim = queries.shape[1]
    upto = (piece + 1) * PIECE
    levels = coeff.shape[1]
    return pl.pallas_call(
        functools.partial(local_kernel, piece),
        out_shape=jax.ShapeDtypeStruct((PIECE, head_dim), jnp.float32),
        grid=(1,),
        in_specs=[
            pl.BlockSpec((PIECE, head_dim), lambda i: (piece, 0)),
            pl.BlockSpec((upto, head_dim), lambda i: (0, 0)),
            pl.BlockSpec((upto, head_dim), lambda i: (0, 0)),
            pl.BlockSpec((PIECE, levels), lambda i: (piece, 0)),
        ],
        out_specs=pl.BlockSpec((PIECE, head_dim), lambda i: (0, 0)),
        compiler_params=pltpu.CompilerParams(vmem_limit_bytes=32 * 1024 * 1024),
        cost_estimate=pl.CostEstimate(
            flops=4 * PIECE * upto * head_dim, bytes_accessed=4 * upto * head_dim, transcendentals=0
        ),
    )(queries, keys, values, coeff)


def finish_kernel(first_level, seq_bits, l0, l1, l2, l3, q_ref, c_ref, hi_ref, lo_ref, out_ref):
    locals_ = (l0, l1, l2, l3)
    for piece in range(4):
        rows = slice(piece * PIECE, (piece + 1) * PIECE)
        q = q_ref[rows, :]
        total = locals_[piece][...]
        cross = jnp.zeros_like(total)
        for j in range(seq_bits):
            readout = dot(q, hi_ref[j]) + dot(q, lo_ref[j])
            level = first_level + j
            cross = cross + readout * c_ref[rows, level : level + 1]
        total = total + cross
        mean = jnp.mean(total * total, axis=1, keepdims=True)
        out_ref[rows, :] = (total * lax.rsqrt(mean + EPSILON)).astype(jnp.bfloat16)


def finish(pieces, queries, coeff, states, first_level):
    hi = states.astype(jnp.bfloat16)
    lo = (states - hi.astype(jnp.float32)).astype(jnp.bfloat16)
    return pl.pallas_call(
        functools.partial(finish_kernel, first_level, states.shape[0]),
        out_shape=jax.ShapeDtypeStruct(queries.shape, jnp.bfloat16),
        compiler_params=pltpu.CompilerParams(vmem_limit_bytes=32 * 1024 * 1024),
        cost_estimate=pl.CostEstimate(
            flops=20 * queries.shape[0] * 128 * 128, bytes_accessed=4 << 20, transcendentals=0
        ),
    )(*pieces, queries, coeff, hi, lo)


def exchange(value):
    size = lax.axis_size("zh")
    own = lax.axis_index("zh")
    rows = value.shape[0] // size
    slots = [lax.dynamic_slice_in_dim(value, own * rows, rows, 0)]
    for apart in range(1, size):
        to = lax.rem(own + apart, size)
        piece = lax.dynamic_slice_in_dim(value, to * rows, rows, 0)
        slots.append(lax.ppermute(piece, "zh", [(i, (i + apart) % size) for i in range(size)]))
    return slots


def exchange_heads(summed):
    size = lax.axis_size("zh")
    own = lax.axis_index("zh")
    sums = [lax.dynamic_index_in_dim(summed, own, 0, keepdims=False)]
    for apart in range(1, size):
        piece = lax.dynamic_index_in_dim(summed, lax.rem(own + apart, size), 0, keepdims=False)
        sums.append(lax.ppermute(piece, "zh", [(i, (i + apart) % size) for i in range(size)]))
    return sums


def line_gather(own):
    size = lax.axis_size("zl")
    up, down = own, own
    ups, downs = {}, {}
    for step in range(1, size):
        up = lax.ppermute(up, "zl", [(i, i + 1) for i in range(step - 1, size - 1)])
        down = lax.ppermute(down, "zl", [(i, i - 1) for i in range(1, size - step + 1)])
        ups[step], downs[step] = up, down
    arrived = [(0, own)]
    for step in range(1, size):
        arrived.append((size - step, ups[step], downs[size - step]))
    return arrived


def level_sums(state):
    size = lax.axis_size("seq")
    index = lax.axis_index("seq")
    sums = []
    for bit in range(size.bit_length() - 1):
        other = lax.ppermute(state, "seq", [(i, i ^ (1 << bit)) for i in range(size)])
        later = jnp.bitwise_and(jnp.right_shift(index, bit), 1) == 1
        sums.append(jnp.where(later, other, 0.0))
        state = state + other
    return jnp.stack(sums)


def product_kernel(slots, away, where_ref, *refs):
    b_refs, a_refs, out_ref = refs[:slots], refs[slots:-1], refs[-1]
    zh, zl = where_ref[0], where_ref[1]
    rows, width = out_ref.shape[-2:]
    b = jnp.concatenate([ref[...] for ref in b_refs], axis=1)
    lines = out_ref.shape[0] // slots
    heads = [lax.rem(zh - d + slots, slots) for d in range(slots)]

    def place(a, d, line):
        product = lax.dot_general(
            a, b, (((0,), (0,)), ((), ())), preferred_element_type=jnp.float32
        ).astype(jnp.bfloat16)
        block = heads[d] * lines + line
        for half in range(2):
            for e in range(slots):
                out_ref[block, half, heads[e]] = product[
                    half * rows : (half + 1) * rows, e * width : (e + 1) * width
                ]

    for d in range(slots):
        place(a_refs[0][d], d, zl)
    for k, distance in enumerate(away):
        line = lax.rem(zl + distance, lines)
        up_ref, down_ref = a_refs[1 + 2 * k], a_refs[2 + 2 * k]
        passed_up = zl >= lines - distance
        for d in range(slots):
            place(jnp.where(passed_up, up_ref[d], down_ref[d]), d, line)


def products(arrived, b_slots):
    slots = len(b_slots)
    rows, width = b_slots[0].shape
    where = jnp.stack([lax.axis_index("zh"), lax.axis_index("zl")]).astype(jnp.int32)
    own, rest = arrived[0][1], arrived[1:]
    operands = [own]
    for _, up, down in rest:
        operands += [up, down]
    smem = pl.BlockSpec(memory_space=pltpu.SMEM)
    vmem = pl.BlockSpec(memory_space=pltpu.VMEM)
    blocks = slots * len(arrived)
    return pl.pallas_call(
        functools.partial(product_kernel, slots, [away for away, *_ in rest]),
        out_shape=jax.ShapeDtypeStruct((blocks, 2, slots, width // 2, width), jnp.bfloat16),
        in_specs=[smem] + [vmem] * (slots + len(operands)),
        out_specs=vmem,
        compiler_params=pltpu.CompilerParams(vmem_limit_bytes=40 * 1024 * 1024),
        cost_estimate=pl.CostEstimate(
            flops=2 * blocks * rows * width * width * slots,
            bytes_accessed=2 * (len(operands) * own.size + slots * rows * width),
            transcendentals=0,
        ),
    )(where, *b_slots, *operands)


def body(queries, keys, values, level_ids, level_table, out_cotangent):
    block_len, head_dim = queries.shape
    n_seq = lax.axis_size("seq")
    local_bits = block_len.bit_length() - 1
    seq_bits = n_seq.bit_length() - 1
    table_rows = level_table.shape[0]
    own_index = lax.axis_index("seq")

    onehot = (level_ids[:, None] == jnp.arange(table_rows, dtype=jnp.int32)[None, :]).astype(
        jnp.float32
    )
    coeff = jnp.dot(onehot, level_table, precision=HIGHEST, preferred_element_type=jnp.float32)
    pieces = [
        local_piece(piece, queries, keys, values, coeff) for piece in range(block_len // PIECE)
    ]

    arrived = line_gather(jnp.stack(exchange(out_cotangent)))

    state = lax.dot_general(
        keys, values, (((0,), (0,)), ((), ())), preferred_element_type=jnp.float32
    )
    level_states = level_sums(state)
    attn_out = finish(pieces, queries, coeff, level_states, local_bits + 1)

    scale = (block_len * n_seq) ** (-0.5)
    partial = products(arrived, exchange(attn_out))
    sent = partial.reshape(n_seq, -1, head_dim)
    summed = lax.all_to_all(sent, "seq", 0, 0, tiled=True).astype(jnp.float32).sum(axis=0)
    summed = summed.reshape(lax.axis_size("zh"), head_dim // 2, head_dim)
    weight_grad = sum(exchange_heads(summed)) * scale
    return attn_out, weight_grad


def solution(mesh):
    n_seq, n_head = mesh.devices.shape
    mesh = jax.sharding.Mesh(
        mesh.devices.reshape(n_seq, n_head // GROUP, GROUP), ("seq", "zh", "zl")
    )
    split = P("seq", ("zh", "zl"))
    return jax.shard_map(
        body,
        mesh=mesh,
        in_specs=(split, split, split, P("seq"), P(), split),
        out_specs=(split, split),
        check_vma=False,
    )
```

```python
import functools

import jax
import jax.numpy as jnp
from jax import lax
from jax.experimental import pallas as pl
from jax.experimental.pallas import tpu as pltpu
from jax.sharding import PartitionSpec as P

EPSILON = 1e-06
HIGHEST = lax.Precision.HIGHEST
PIECE = 512
TILE = 128
GROUP = 2


def dot_t(a, b):
    return lax.dot_general(a, b, (((1,), (1,)), ((), ())), preferred_element_type=jnp.float32)


def dot(a, b):
    return jnp.dot(a, b, preferred_element_type=jnp.float32)


def local_kernel(piece, q_ref, k_ref, v_ref, c_ref, out_ref):
    base = piece * PIECE
    piece_bits = PIECE.bit_length() - 1
    tile_bits = TILE.bit_length() - 1
    q = q_ref[...]
    total = jnp.zeros((PIECE, q.shape[1]), jnp.float32)
    first = 0
    for bit in reversed(range(max(piece.bit_length(), 1))):
        if not (piece >> bit) & 1:
            continue
        last = first + (PIECE << bit)
        level = piece_bits + bit + 1
        scores = dot_t(q, k_ref[first:last, :])
        mixed = (scores * c_ref[:, level : level + 1]).astype(jnp.bfloat16)
        total = total + dot(mixed, v_ref[first:last, :])
        first = last
    out_ref[...] = total
    for bit in reversed(range(piece_bits - tile_bits)):
        half = TILE << bit
        level = tile_bits + bit + 1
        for start in range(0, PIECE, 2 * half):
            rows = slice(start + half, start + 2 * half)
            cols = slice(base + start, base + start + half)
            scores = dot_t(q_ref[rows, :], k_ref[cols, :])
            mixed = (scores * c_ref[rows, level : level + 1]).astype(jnp.bfloat16)
            out_ref[rows, :] += dot(mixed, v_ref[cols, :])
    row = lax.broadcasted_iota(jnp.int32, (TILE, TILE), 0)
    col = lax.broadcasted_iota(jnp.int32, (TILE, TILE), 1)
    apart = jnp.bitwise_xor(row, col)
    causal = col <= row
    for start in range(0, PIECE, TILE):
        rows = slice(start, start + TILE)
        cols = slice(base + start, base + start + TILE)
        weights = jnp.broadcast_to(c_ref[rows, 0:1], (TILE, TILE))
        for level in range(1, tile_bits + 1):
            weights = jnp.where(apart >= 1 << (level - 1), c_ref[rows, level : level + 1], weights)
        weights = jnp.where(causal, weights, 0.0)
        mixed = (dot_t(q_ref[rows, :], k_ref[cols, :]) * weights).astype(jnp.bfloat16)
        out_ref[rows, :] += dot(mixed, v_ref[cols, :])


def local_piece(piece, queries, keys, values, coeff):
    head_dim = queries.shape[1]
    upto = (piece + 1) * PIECE
    levels = coeff.shape[1]
    return pl.pallas_call(
        functools.partial(local_kernel, piece),
        out_shape=jax.ShapeDtypeStruct((PIECE, head_dim), jnp.float32),
        grid=(1,),
        in_specs=[
            pl.BlockSpec((PIECE, head_dim), lambda i: (piece, 0)),
            pl.BlockSpec((upto, head_dim), lambda i: (0, 0)),
            pl.BlockSpec((upto, head_dim), lambda i: (0, 0)),
            pl.BlockSpec((PIECE, levels), lambda i: (piece, 0)),
        ],
        out_specs=pl.BlockSpec((PIECE, head_dim), lambda i: (0, 0)),
        compiler_params=pltpu.CompilerParams(vmem_limit_bytes=32 * 1024 * 1024),
        cost_estimate=pl.CostEstimate(
            flops=4 * PIECE * upto * head_dim, bytes_accessed=4 * upto * head_dim, transcendentals=0
        ),
    )(queries, keys, values, coeff)


def finish_kernel(first_level, seq_bits, l0, l1, l2, l3, q_ref, c_ref, hi_ref, lo_ref, out_ref):
    locals_ = (l0, l1, l2, l3)
    for piece in range(4):
        rows = slice(piece * PIECE, (piece + 1) * PIECE)
        q = q_ref[rows, :]
        total = locals_[piece][...]
        cross = jnp.zeros_like(total)
        for j in range(seq_bits):
            readout = dot(q, hi_ref[j]) + dot(q, lo_ref[j])
            level = first_level + j
            cross = cross + readout * c_ref[rows, level : level + 1]
        total = total + cross
        mean = jnp.mean(total * total, axis=1, keepdims=True)
        out_ref[rows, :] = (total * lax.rsqrt(mean + EPSILON)).astype(jnp.bfloat16)


def finish(pieces, queries, coeff, states, first_level):
    hi = states.astype(jnp.bfloat16)
    lo = (states - hi.astype(jnp.float32)).astype(jnp.bfloat16)
    return pl.pallas_call(
        functools.partial(finish_kernel, first_level, states.shape[0]),
        out_shape=jax.ShapeDtypeStruct(queries.shape, jnp.bfloat16),
        compiler_params=pltpu.CompilerParams(vmem_limit_bytes=32 * 1024 * 1024),
        cost_estimate=pl.CostEstimate(
            flops=20 * queries.shape[0] * 128 * 128, bytes_accessed=4 << 20, transcendentals=0
        ),
    )(*pieces, queries, coeff, hi, lo)


def exchange(value):
    size = lax.axis_size("zl")
    own = lax.axis_index("zl")
    rows = value.shape[0] // size
    slots = [lax.dynamic_slice_in_dim(value, own * rows, rows, 0)]
    for apart in range(1, size):
        to = lax.rem(own + apart, size)
        piece = lax.dynamic_slice_in_dim(value, to * rows, rows, 0)
        slots.append(lax.ppermute(piece, "zl", [(i, (i + apart) % size) for i in range(size)]))
    return slots


def ring_gather(slots, hold):
    size = lax.axis_size("zh")
    right = [(i, (i + 1) % size) for i in range(size)]
    left = [(i, (i - 1) % size) for i in range(size)]
    ups, downs = list(slots), list(slots)
    arrived = [(0, slot, value) for slot, value in enumerate(slots)]
    for step in range(1, size // 2):
        for slot in range(len(slots)):
            up = lax.ppermute(ups[slot], "zh", right)
            down = lax.ppermute(downs[slot], "zh", left)
            up, down = hold(step, slot, up, down)
            arrived += [(size - step, slot, up), (step, slot, down)]
            ups[slot], downs[slot] = up, down
    for slot in range(len(slots)):
        source, way = (ups, right) if slot % 2 == 0 else (downs, left)
        arrived.append((size // 2, slot, lax.ppermute(source[slot], "zh", way)))
    return arrived


class LevelSums:
    def __init__(self):
        self.state = None
        self.sums = []

    def step(self, *beside):
        size = lax.axis_size("seq")
        bit = len(self.sums)
        if 1 << bit >= size:
            return beside
        self.state, *beside = lax.optimization_barrier((self.state, *beside))
        other = lax.ppermute(self.state, "seq", [(i, i ^ (1 << bit)) for i in range(size)])
        later = jnp.bitwise_and(jnp.right_shift(lax.axis_index("seq"), bit), 1) == 1
        self.sums.append(jnp.where(later, other, 0.0))
        self.state = self.state + other
        return beside

    def finish(self):
        while 1 << len(self.sums) < lax.axis_size("seq"):
            self.step()
        return jnp.stack(self.sums)


def product_store(place, count, blocks, zh, zl, a_refs, b_refs, store):
    b = jnp.concatenate([ref[...] for ref in b_refs], axis=1)
    for (away, first, slots), a_ref in zip(blocks, a_refs):
        group = lax.rem(zh + away, count)
        for slot in range(slots):
            a = a_ref[...]
            product = lax.dot_general(
                a, b, (((0,), (0,)), ((), ())), preferred_element_type=jnp.float32
            ).astype(jnp.bfloat16)
            block = group * place + lax.rem(zl - (first + slot) + place, place)
            store(block, product)


def early_kernel(place, count, blocks, where_ref, *refs):
    b_refs, a_refs, out_ref = refs[:place], refs[place:-1], refs[-1]
    done = [0]

    def store(block, product):
        out_ref[done[0]] = product
        done[0] += 1

    product_store(place, count, blocks, where_ref[0], where_ref[1], a_refs, b_refs, store)


def late_kernel(place, count, early_blocks, blocks, where_ref, early_ref, *refs):
    b_refs, a_refs, out_ref = refs[:place], refs[place:-1], refs[-1]
    zh, zl = where_ref[0], where_ref[1]
    width = out_ref.shape[-1]
    rows = out_ref.shape[-2]

    def store(block, product):
        for half in range(2):
            for d in range(place):
                head = lax.rem(zl - d + place, place)
                out_ref[block, half, head] = product[
                    half * rows : (half + 1) * rows, d * width : (d + 1) * width
                ]

    done = 0
    for away, first, slots in early_blocks:
        group = lax.rem(zh + away, count)
        for slot in range(slots):
            block = group * place + lax.rem(zl - (first + slot) + place, place)
            store(block, early_ref[done])
            done += 1
    product_store(place, count, blocks, zh, zl, a_refs, b_refs, store)


def product_cost(blocks, shape, place):
    count = sum(slots for _, _, slots in blocks)
    rows, width = shape
    return pl.CostEstimate(
        flops=2 * count * rows * width * width * place,
        bytes_accessed=2 * rows * width * (count + place),
        transcendentals=0,
    )


def products(early, late, b_slots, zh_count):
    place = len(b_slots)
    rows, width = b_slots[0].shape
    where = jnp.stack([lax.axis_index("zh"), lax.axis_index("zl")]).astype(jnp.int32)
    early_blocks = [(away, first, 1) for away, first, _ in early]
    late_blocks = [(away, first, 1) for away, first, _ in late]
    count = sum(slots for _, _, slots in early_blocks)
    smem = pl.BlockSpec(memory_space=pltpu.SMEM)
    vmem = pl.BlockSpec(memory_space=pltpu.VMEM)
    params = pltpu.CompilerParams(vmem_limit_bytes=40 * 1024 * 1024)
    first = pl.pallas_call(
        functools.partial(early_kernel, place, zh_count, early_blocks),
        out_shape=jax.ShapeDtypeStruct((count, width, place * width), jnp.bfloat16),
        in_specs=[smem] + [vmem] * (place + len(early)),
        out_specs=vmem,
        compiler_params=params,
        cost_estimate=product_cost(early_blocks, (rows, width), place),
    )(where, *b_slots, *[a for _, _, a in early])
    return pl.pallas_call(
        functools.partial(late_kernel, place, zh_count, early_blocks, late_blocks),
        out_shape=jax.ShapeDtypeStruct(
            (zh_count * place, 2, place, width // 2, width), jnp.bfloat16
        ),
        in_specs=[smem] + [vmem] * (1 + place + len(late)),
        out_specs=vmem,
        compiler_params=params,
        cost_estimate=product_cost(late_blocks, (rows, width), place),
    )(where, first, *b_slots, *[a for _, _, a in late])


def body(queries, keys, values, level_ids, level_table, out_cotangent):
    block_len, head_dim = queries.shape
    n_seq = lax.axis_size("seq")
    local_bits = block_len.bit_length() - 1
    seq_bits = n_seq.bit_length() - 1
    table_rows = level_table.shape[0]
    own_index = lax.axis_index("seq")

    onehot = (level_ids[:, None] == jnp.arange(table_rows, dtype=jnp.int32)[None, :]).astype(
        jnp.float32
    )
    coeff = jnp.dot(onehot, level_table, precision=HIGHEST, preferred_element_type=jnp.float32)
    pieces = [
        local_piece(piece, queries, keys, values, coeff) for piece in range(block_len // PIECE)
    ]

    slots = exchange(out_cotangent)
    *slots[1:], pieces[0] = lax.optimization_barrier((*slots[1:], pieces[0]))
    level_sums = LevelSums()

    def hold(step, slot, up, down):
        if (step, slot) == (1, 0):
            up, down, *rest = lax.optimization_barrier((up, down, keys, values))
            level_sums.state = lax.dot_general(
                *rest, (((0,), (0,)), ((), ())), preferred_element_type=jnp.float32
            )
            level_sums.step()
        elif (step, slot) in ((1, 1), (2, 0), (2, 1)):
            (up,) = level_sums.step(up)
            if (step, slot) == (2, 0):
                (down,) = level_sums.step(down)
        return up, down

    blocks = ring_gather(slots, hold)
    level_states = level_sums.finish()
    attn_out = finish(pieces, queries, coeff, level_states, local_bits + 1)

    scale = (block_len * n_seq) ** (-0.5)
    late = 6
    partial = products(blocks[:-late], blocks[-late:], exchange(attn_out), lax.axis_size("zh"))
    sent = partial.reshape(-1, head_dim // 2, head_dim)
    arrived = lax.all_to_all(sent, ("seq", "zl"), 0, 0, tiled=True)
    weight_grad = arrived.astype(jnp.float32).sum(axis=0) * scale
    return attn_out, weight_grad


def solution(mesh):
    n_seq, n_head = mesh.devices.shape
    mesh = jax.sharding.Mesh(
        mesh.devices.reshape(n_seq, n_head // GROUP, GROUP), ("seq", "zh", "zl")
    )
    split = P("seq", ("zh", "zl"))
    return jax.shard_map(
        body,
        mesh=mesh,
        in_specs=(split, split, split, P("seq"), P(), split),
        out_specs=(split, split),
        check_vma=False,
    )
```

```python
import functools

import jax
import jax.numpy as jnp
from jax import lax
from jax.experimental import pallas as pl
from jax.experimental.pallas import tpu as pltpu
from jax.sharding import PartitionSpec as P

EPSILON = 1e-06
HIGHEST = lax.Precision.HIGHEST
PIECE = 512
TILE = 128
GROUP = 2


def dot_t(a, b):
    return lax.dot_general(a, b, (((1,), (1,)), ((), ())), preferred_element_type=jnp.float32)


def dot(a, b):
    return jnp.dot(a, b, preferred_element_type=jnp.float32)


def local_kernel(piece, q_ref, k_ref, v_ref, c_ref, out_ref):
    base = piece * PIECE
    piece_bits = PIECE.bit_length() - 1
    tile_bits = TILE.bit_length() - 1
    q = q_ref[...]
    total = jnp.zeros((PIECE, q.shape[1]), jnp.float32)
    first = 0
    for bit in reversed(range(max(piece.bit_length(), 1))):
        if not (piece >> bit) & 1:
            continue
        last = first + (PIECE << bit)
        level = piece_bits + bit + 1
        scores = dot_t(q, k_ref[first:last, :])
        mixed = (scores * c_ref[:, level : level + 1]).astype(jnp.bfloat16)
        total = total + dot(mixed, v_ref[first:last, :])
        first = last
    out_ref[...] = total
    for bit in reversed(range(piece_bits - tile_bits)):
        half = TILE << bit
        level = tile_bits + bit + 1
        for start in range(0, PIECE, 2 * half):
            rows = slice(start + half, start + 2 * half)
            cols = slice(base + start, base + start + half)
            scores = dot_t(q_ref[rows, :], k_ref[cols, :])
            mixed = (scores * c_ref[rows, level : level + 1]).astype(jnp.bfloat16)
            out_ref[rows, :] += dot(mixed, v_ref[cols, :])
    row = lax.broadcasted_iota(jnp.int32, (TILE, TILE), 0)
    col = lax.broadcasted_iota(jnp.int32, (TILE, TILE), 1)
    apart = jnp.bitwise_xor(row, col)
    causal = col <= row
    for start in range(0, PIECE, TILE):
        rows = slice(start, start + TILE)
        cols = slice(base + start, base + start + TILE)
        weights = jnp.broadcast_to(c_ref[rows, 0:1], (TILE, TILE))
        for level in range(1, tile_bits + 1):
            weights = jnp.where(apart >= 1 << (level - 1), c_ref[rows, level : level + 1], weights)
        weights = jnp.where(causal, weights, 0.0)
        mixed = (dot_t(q_ref[rows, :], k_ref[cols, :]) * weights).astype(jnp.bfloat16)
        out_ref[rows, :] += dot(mixed, v_ref[cols, :])


def local_piece(piece, queries, keys, values, coeff):
    head_dim = queries.shape[1]
    upto = (piece + 1) * PIECE
    levels = coeff.shape[1]
    return pl.pallas_call(
        functools.partial(local_kernel, piece),
        out_shape=jax.ShapeDtypeStruct((PIECE, head_dim), jnp.float32),
        grid=(1,),
        in_specs=[
            pl.BlockSpec((PIECE, head_dim), lambda i: (piece, 0)),
            pl.BlockSpec((upto, head_dim), lambda i: (0, 0)),
            pl.BlockSpec((upto, head_dim), lambda i: (0, 0)),
            pl.BlockSpec((PIECE, levels), lambda i: (piece, 0)),
        ],
        out_specs=pl.BlockSpec((PIECE, head_dim), lambda i: (0, 0)),
        compiler_params=pltpu.CompilerParams(vmem_limit_bytes=32 * 1024 * 1024),
        cost_estimate=pl.CostEstimate(
            flops=4 * PIECE * upto * head_dim, bytes_accessed=4 * upto * head_dim, transcendentals=0
        ),
    )(queries, keys, values, coeff)


def finish_kernel(first_level, seq_bits, l0, l1, l2, l3, q_ref, c_ref, hi_ref, lo_ref, out_ref):
    locals_ = (l0, l1, l2, l3)
    for piece in range(4):
        rows = slice(piece * PIECE, (piece + 1) * PIECE)
        q = q_ref[rows, :]
        total = locals_[piece][...]
        cross = jnp.zeros_like(total)
        for j in range(seq_bits):
            readout = dot(q, hi_ref[j]) + dot(q, lo_ref[j])
            level = first_level + j
            cross = cross + readout * c_ref[rows, level : level + 1]
        total = total + cross
        mean = jnp.mean(total * total, axis=1, keepdims=True)
        out_ref[rows, :] = (total * lax.rsqrt(mean + EPSILON)).astype(jnp.bfloat16)


def finish(pieces, queries, coeff, states, first_level):
    hi = states.astype(jnp.bfloat16)
    lo = (states - hi.astype(jnp.float32)).astype(jnp.bfloat16)
    return pl.pallas_call(
        functools.partial(finish_kernel, first_level, states.shape[0]),
        out_shape=jax.ShapeDtypeStruct(queries.shape, jnp.bfloat16),
        compiler_params=pltpu.CompilerParams(vmem_limit_bytes=32 * 1024 * 1024),
        cost_estimate=pl.CostEstimate(
            flops=20 * queries.shape[0] * 128 * 128, bytes_accessed=4 << 20, transcendentals=0
        ),
    )(*pieces, queries, coeff, hi, lo)


def exchange(value):
    size = lax.axis_size("zl")
    own = lax.axis_index("zl")
    rows = value.shape[0] // size
    slots = [lax.dynamic_slice_in_dim(value, own * rows, rows, 0)]
    for apart in range(1, size):
        to = lax.rem(own + apart, size)
        piece = lax.dynamic_slice_in_dim(value, to * rows, rows, 0)
        slots.append(lax.ppermute(piece, "zl", [(i, (i + apart) % size) for i in range(size)]))
    return slots


def ring_gather(slots, hold):
    size = lax.axis_size("zh")
    right = [(i, (i + 1) % size) for i in range(size)]
    left = [(i, (i - 1) % size) for i in range(size)]
    ups, downs = list(slots), list(slots)
    arrived = [(0, slot, value) for slot, value in enumerate(slots)]
    for step in range(1, size // 2):
        for slot in range(len(slots)):
            up = lax.ppermute(ups[slot], "zh", right)
            down = lax.ppermute(downs[slot], "zh", left)
            up, down = hold(step, slot, up, down)
            arrived += [(size - step, slot, up), (step, slot, down)]
            ups[slot], downs[slot] = up, down
    for slot in range(len(slots)):
        source, way = (ups, right) if slot % 2 == 0 else (downs, left)
        arrived.append((size // 2, slot, lax.ppermute(source[slot], "zh", way)))
    return arrived


class LevelSums:
    def __init__(self):
        self.state = None
        self.sums = []

    def step(self, *beside):
        size = lax.axis_size("seq")
        bit = len(self.sums)
        if 1 << bit >= size:
            return beside
        self.state, *beside = lax.optimization_barrier((self.state, *beside))
        other = lax.ppermute(self.state, "seq", [(i, i ^ (1 << bit)) for i in range(size)])
        later = jnp.bitwise_and(jnp.right_shift(lax.axis_index("seq"), bit), 1) == 1
        self.sums.append(jnp.where(later, other, 0.0))
        self.state = self.state + other
        return beside

    def finish(self):
        while 1 << len(self.sums) < lax.axis_size("seq"):
            self.step()
        return jnp.stack(self.sums)


def product_store(place, count, blocks, zh, zl, a_refs, b_refs, store):
    b = jnp.concatenate([ref[...] for ref in b_refs], axis=1)
    for (away, first, slots), a_ref in zip(blocks, a_refs):
        group = lax.rem(zh + away, count)
        for slot in range(slots):
            a = a_ref[...]
            product = lax.dot_general(
                a, b, (((0,), (0,)), ((), ())), preferred_element_type=jnp.float32
            ).astype(jnp.bfloat16)
            block = group * place + lax.rem(zl - (first + slot) + place, place)
            store(block, product)


def early_kernel(place, count, blocks, where_ref, *refs):
    b_refs, a_refs, out_ref = refs[:place], refs[place:-1], refs[-1]
    done = [0]

    def store(block, product):
        out_ref[done[0]] = product
        done[0] += 1

    product_store(place, count, blocks, where_ref[0], where_ref[1], a_refs, b_refs, store)


def late_kernel(place, count, early_blocks, blocks, where_ref, early_ref, *refs):
    b_refs, a_refs, out_ref = refs[:place], refs[place:-1], refs[-1]
    zh, zl = where_ref[0], where_ref[1]
    width = out_ref.shape[-1]
    rows = out_ref.shape[-2]

    def store(block, product):
        for half in range(2):
            for d in range(place):
                head = lax.rem(zl - d + place, place)
                out_ref[block, half, head] = product[
                    half * rows : (half + 1) * rows, d * width : (d + 1) * width
                ]

    done = 0
    for away, first, slots in early_blocks:
        group = lax.rem(zh + away, count)
        for slot in range(slots):
            block = group * place + lax.rem(zl - (first + slot) + place, place)
            store(block, early_ref[done])
            done += 1
    product_store(place, count, blocks, zh, zl, a_refs, b_refs, store)


def product_cost(blocks, shape, place):
    count = sum(slots for _, _, slots in blocks)
    rows, width = shape
    return pl.CostEstimate(
        flops=2 * count * rows * width * width * place,
        bytes_accessed=2 * rows * width * (count + place),
        transcendentals=0,
    )


def products(early, late, b_slots, zh_count):
    place = len(b_slots)
    rows, width = b_slots[0].shape
    where = jnp.stack([lax.axis_index("zh"), lax.axis_index("zl")]).astype(jnp.int32)
    early_blocks = [(away, first, 1) for away, first, _ in early]
    late_blocks = [(away, first, 1) for away, first, _ in late]
    count = sum(slots for _, _, slots in early_blocks)
    smem = pl.BlockSpec(memory_space=pltpu.SMEM)
    vmem = pl.BlockSpec(memory_space=pltpu.VMEM)
    params = pltpu.CompilerParams(vmem_limit_bytes=40 * 1024 * 1024)
    first = pl.pallas_call(
        functools.partial(early_kernel, place, zh_count, early_blocks),
        out_shape=jax.ShapeDtypeStruct((count, width, place * width), jnp.bfloat16),
        in_specs=[smem] + [vmem] * (place + len(early)),
        out_specs=vmem,
        compiler_params=params,
        cost_estimate=product_cost(early_blocks, (rows, width), place),
    )(where, *b_slots, *[a for _, _, a in early])
    return pl.pallas_call(
        functools.partial(late_kernel, place, zh_count, early_blocks, late_blocks),
        out_shape=jax.ShapeDtypeStruct(
            (zh_count * place, 2, place, width // 2, width), jnp.bfloat16
        ),
        in_specs=[smem] + [vmem] * (1 + place + len(late)),
        out_specs=vmem,
        compiler_params=params,
        cost_estimate=product_cost(late_blocks, (rows, width), place),
    )(where, first, *b_slots, *[a for _, _, a in late])


def body(queries, keys, values, level_ids, level_table, out_cotangent):
    block_len, head_dim = queries.shape
    n_seq = lax.axis_size("seq")
    local_bits = block_len.bit_length() - 1
    seq_bits = n_seq.bit_length() - 1
    table_rows = level_table.shape[0]
    own_index = lax.axis_index("seq")

    onehot = (level_ids[:, None] == jnp.arange(table_rows, dtype=jnp.int32)[None, :]).astype(
        jnp.float32
    )
    coeff = jnp.dot(onehot, level_table, precision=HIGHEST, preferred_element_type=jnp.float32)
    pieces = [
        local_piece(piece, queries, keys, values, coeff) for piece in range(block_len // PIECE)
    ]

    slots = exchange(out_cotangent)
    slots[0], *slots[1:] = lax.optimization_barrier(tuple(slots))
    level_sums = LevelSums()

    def hold(step, slot, up, down):
        if (step, slot) == (1, 0):
            up, down, *rest = lax.optimization_barrier((up, down, keys, values))
            level_sums.state = lax.dot_general(
                *rest, (((0,), (0,)), ((), ())), preferred_element_type=jnp.float32
            )
            level_sums.step()
        elif (step, slot) in ((1, 1), (2, 0), (2, 1)):
            (up,) = level_sums.step(up)
            if (step, slot) == (2, 0):
                (down,) = level_sums.step(down)
        return up, down

    blocks = ring_gather(slots, hold)
    level_states = level_sums.finish()
    attn_out = finish(pieces, queries, coeff, level_states, local_bits + 1)

    scale = (block_len * n_seq) ** (-0.5)
    late = 6
    partial = products(blocks[:-late], blocks[-late:], exchange(attn_out), lax.axis_size("zh"))
    sent = partial.reshape(-1, head_dim // 2, head_dim)
    arrived = lax.all_to_all(sent, ("seq", "zl"), 0, 0, tiled=True)
    weight_grad = arrived.astype(jnp.float32).sum(axis=0) * scale
    return attn_out, weight_grad


def solution(mesh):
    n_seq, n_head = mesh.devices.shape
    mesh = jax.sharding.Mesh(
        mesh.devices.reshape(n_seq, n_head // GROUP, GROUP), ("seq", "zh", "zl")
    )
    split = P("seq", ("zh", "zl"))
    return jax.shard_map(
        body,
        mesh=mesh,
        in_specs=(split, split, split, P("seq"), P(), split),
        out_specs=(split, split),
        check_vma=False,
    )
```
